32 devices in a mesh: dp: 16 (over z, y, core), patch: 2 (over x).
Axes of the slice: x: 2, y: 2, z: 4, core: 2. Of those that a mesh axis runs over, the one named last changes fastest.
Arguments:
- hidden: bfloat16 [64, 256, 768], P(('dp', 'patch')), may hold values from -6 to 6
- lengths: int32 [64, 4], P(('dp', 'patch')), may hold values from 1 to 64, 128 in all within a row
- image_order: int32 [64, 4], P(('dp', 'patch')), may hold values from 0 to 3, each once within a row
- features: bfloat16 [64, 4, 264, 1408], P('dp', None, 'patch'), may hold values from -6 to 6
- cotangent: bfloat16 [64, 256, 768], P(('dp', 'patch')), may hold values from -6 to 6
- self_weight: bfloat16 [768, 2304], replicated, may hold values from -0.21875 to 0.21875
- output_weight: bfloat16 [768, 768], replicated, may hold values from -0.875 to 0.875
- self_bias: float32 [3, 768], replicated, may hold values from -2 to 2
- norm_gain: float32 [4, 768], replicated, may hold values from 0.5 to 1.5
- norm_shift: float32 [4, 768], replicated, may hold values from -2 to 2
- query_weight: bfloat16 [768, 768], replicated, may hold values from -0.21875 to 0.21875
- image_weight: bfloat16 [1408, 1536], replicated, may hold values from -0.15625 to 0.15625
- cross_weight: bfloat16 [768, 768], replicated, may hold values from -1.75 to 1.75
- cross_bias: float32 [3, 768], replicated, may hold values from -2 to 2
- expand_weight: bfloat16 [768, 6144], replicated, may hold values from -0.21875 to 0.21875
- expand_bias: float32 [6144], replicated, may hold values from -2 to 2
- reduce_weight: bfloat16 [6144, 768], replicated, may hold values from -0.109375 to 0.109375
- reduce_bias: float32 [2, 768], replicated, may hold values from -2 to 2
Outputs:
- mixed: bfloat16 [64, 256, 768], P(('dp', 'patch'))
- hidden_gradient: bfloat16 [64, 256, 768], P(('dp', 'patch'))
- self_weight_gradient: float32 [768, 2304], P('dp', 'patch')
- output_weight_gradient: float32 [768, 768], P('dp', 'patch')
- self_bias_gradient: float32 [3, 768], replicated
- norm_gain_gradient: float32 [4, 768], replicated
- norm_shift_gradient: float32 [4, 768], replicated
- query_weight_gradient: float32 [768, 768], P('dp', 'patch')
- image_weight_gradient: float32 [1408, 1536], P('dp', 'patch')
- cross_weight_gradient: float32 [768, 768], P('dp', 'patch')
- cross_bias_gradient: float32 [3, 768], replicated
- expand_weight_gradient: float32 [768, 6144], P('dp', 'patch')
- expand_bias_gradient: float32 [6144], replicated
- reduce_weight_gradient: float32 [6144, 768], P('dp', 'patch')
- reduce_bias_gradient: float32 [2, 768], replicated
The draws below stay inside these ranges and needn't reach their ends.
Inputs may be any that keep to these rules, and one draw needn't show every extreme that they name: `lengths`: the 4 captions of a row together fill its 128 caption tokens, and the longest caption of every row has exactly 64 tokens. `image_order`: each row names each of its 4 images once.
All inputs are finite; a program needn't handle non-finite values.
Results may differ from the reference program's by a relative error of at most 0.025.
Values may be sent and summed in bfloat16 or wider, within the bound.
A program may use at most 320 MiB of HBM per device.

```python
import math
import jax
import jax.numpy as jnp
import numpy as np
from jax import lax

D = 768
HEADS = 12
FF = 3072
IMAGE_WIDTH = 1408
QUERIES = 32
GROUPS = 4
TEXT = 128
MOST = 64
PATCHES = 264
PAD = 7
SEQ = 256
ROWS = 64


def spiked(array, own_key, source, target, shards_of, factor):
    owner, partner = [(jnp.arange(array.shape[position]) // (array.shape[position] // shards_of)).reshape([-1 if axis == position else 1 for axis in range(array.ndim)]) for position in (source, target)]
    chosen = jax.random.permutation(own_key, shards_of)[partner]
    strong = (owner == chosen) | (owner == (partner + shards_of // 2) % shards_of)
    return jnp.where(strong, factor * array, array)


def block_scale(rng, shape, pieces, smallest, top_value):
    def one(position, shards_of):
        steps = jax.random.uniform(jax.random.fold_in(jax.random.fold_in(rng, 6), position), (shards_of,), jnp.float32, smallest / len(pieces), top_value / len(pieces))
        return jnp.repeat(jnp.exp(steps), shape[position] // shards_of).reshape((-1,) + (1,) * (len(shape) - position - 1))

    gain = one(*pieces[0])
    for cut in pieces[1:]:
        gain = gain * one(*cut)
    return gain


def split_up(count, total, bound, skew):
    portions = [(1 << 20) // math.isqrt(grade ** skew) + 1 for grade in range(2, count + 1)]
    surplus, holding = total - bound - (count - 1), [1] * (count - 1)
    while surplus > 0:
        free = [i for i in range(count - 1) if holding[i] < bound]
        whole, budget = sum([portions[i] for i in free]), surplus
        for i in free:
            more = min(bound - holding[i], max(1, budget * portions[i] // whole), surplus)
            holding[i] = holding[i] + more
            surplus = surplus - more
    return np.array([bound] + holding)


def uneven(stream_key, amount, total, reach, skew):
    if amount == 2:
        one = jax.random.randint(stream_key, (), max(1, total - reach), min(reach, total - 1) + 1)
        return jnp.stack([one, total - one])
    tallies = jnp.asarray(split_up(amount, total, reach, skew), jnp.int32)
    pairs = (amount - 1) // 2
    donor, receiver = tallies[1:1 + 2 * pairs:2], tallies[2:2 + 2 * pairs:2]
    room = jnp.minimum(donor - 1, reach - receiver)
    moved = jax.random.randint(jax.random.fold_in(stream_key, 1), (pairs,), 0, 1 << 20) % (room + 1)
    tallies = tallies.at[1:1 + 2 * pairs:2].set(donor - moved).at[2:2 + 2 * pairs:2].set(receiver + moved)
    return tallies[jax.random.permutation(jax.random.fold_in(stream_key, 2), amount)]


def gaussian(stream_key, dims, spread, bound, cuts=(), kind=jnp.bfloat16):
    entries = spread * jax.random.normal(stream_key, dims, jnp.float32)
    if cuts:
        entries = entries * block_scale(stream_key, dims, cuts, -0.22, 0.18)
    return jnp.clip(entries, -bound, bound).astype(kind)


def bell_draw_with(own_key, extent, scale, limit, pieces, heavy, held_as=jnp.bfloat16):
    values = scale * jax.random.normal(own_key, extent, jnp.float32)
    if pieces:
        values = values * block_scale(own_key, extent, pieces, -0.22, 0.18)
    return jnp.clip(spiked(values, jax.random.fold_in(own_key, 3), *heavy), -limit, limit).astype(held_as)


def setup_inputs(seed: int = 0) -> dict:
    streams_of = jax.random.split(jax.random.key(seed), 19)
    return {
        "hidden": gaussian(streams_of[0], (ROWS, SEQ, D), 1.0, 6.0, ((0, 32),)),
        "lengths": jax.vmap(lambda own: uneven(own, GROUPS, TEXT, MOST, 1))(jax.random.split(streams_of[1], ROWS)).reshape((ROWS, GROUPS)).astype(jnp.int32),
        "image_order": jax.vmap(lambda own: jax.random.permutation(own, GROUPS))(jax.random.split(streams_of[2], ROWS)).reshape((ROWS, GROUPS)).astype(jnp.int32),
        "features": gaussian(streams_of[3], (ROWS, GROUPS, PATCHES, IMAGE_WIDTH), 1.0, 6.0, ((0, 16), (2, 2))),
        "cotangent": bell_draw_with(streams_of[4], (ROWS, SEQ, D), 1.0, 6.0, ((0, 32),), (0, 2, 32, 2.75)),
        "self_weight": gaussian(streams_of[5], (D, 3 * D), D ** -0.5, 0.21875),
        "output_weight": gaussian(streams_of[6], (D, D), (max(D // 16, 1)) ** -0.5, 0.875),
        "self_bias": gaussian(streams_of[7], (3, D), 0.3, 2.0, (), jnp.float32),
        "norm_gain": jnp.clip(1.0 + 0.1 * jax.random.normal(streams_of[8], (4, D), jnp.float32), 0.5, 1.5),
        "norm_shift": gaussian(streams_of[9], (4, D), 0.3, 2.0, (), jnp.float32),
        "query_weight": gaussian(streams_of[10], (D, D), D ** -0.5, 0.21875),
        "image_weight": gaussian(streams_of[11], (IMAGE_WIDTH, 2 * D), IMAGE_WIDTH ** -0.5, 0.15625),
        "cross_weight": gaussian(streams_of[12], (D, D), (max(D // 64, 1)) ** -0.5, 1.75),
        "cross_bias": gaussian(streams_of[13], (3, D), 0.3, 2.0, (), jnp.float32),
        "expand_weight": gaussian(streams_of[14], (D, 2 * FF), D ** -0.5, 0.21875),
        "expand_bias": gaussian(streams_of[15], (2 * FF,), 0.3, 2.0, (), jnp.float32),
        "reduce_weight": gaussian(streams_of[16], (2 * FF, D), FF ** -0.5, 0.109375),
        "reduce_bias": gaussian(streams_of[17], (2, D), 0.3, 2.0, (), jnp.float32),
    }


highest = lax.Precision.HIGHEST
epsilon = 1e-06
masked_score = -1000000000.0

@jax.custom_vjp
def low(v):
    return lax.optimization_barrier(v.astype(jnp.bfloat16)).astype(jnp.float32)

@jax.custom_vjp
def low_back(v):
    return v

def low_keep(v):
    return (low(v), None)

def low_pass(kept, grad):
    return (grad,)

def back_keep(v):
    return (v, None)

def back_low(kept, grad):
    return (low(grad),)
low.defvjp(low_keep, low_pass)
low_back.defvjp(back_keep, back_low)

def segments(lengths):
    group_ends = jnp.cumsum(lengths, axis=-1, dtype=jnp.int32)
    text_place = jnp.arange(TEXT, dtype=jnp.int32)
    text_group = lax.optimization_barrier(jnp.sum((group_ends[:, None, :] <= text_place[None, :, None]).astype(jnp.int32), axis=-1, dtype=jnp.int32))
    query_group = jnp.arange(GROUPS * QUERIES, dtype=jnp.int32) // QUERIES
    query_group = jnp.broadcast_to(query_group[None, :], (lengths.shape[0], GROUPS * QUERIES))
    return jnp.concatenate([query_group, text_group], axis=1)

def layer_norm(hidden, scales, shifts):
    row_mean = lax.optimization_barrier(jnp.mean(hidden, axis=-1, keepdims=True))
    centered = hidden - row_mean
    variance = lax.optimization_barrier(jnp.mean(centered * centered, axis=-1, keepdims=True))
    return centered * lax.rsqrt(variance + epsilon) * scales + shifts

def linear(inputs, weight):
    return jnp.einsum('...i,ij->...j', inputs, weight, precision=highest)

def heads_of(tensor):
    return tensor.reshape(tensor.shape[:-1] + (HEADS, D // HEADS))

def layer(params, hidden, segment, image_order, images):
    self_weight, output_weight, self_bias, norm_gain, norm_shift, query_weight, image_weight, cross_weight, cross_bias, expand_weight, expand_bias, reduce_weight, reduce_bias = params
    score_scale = (D // HEADS) ** (-0.5)
    batch_rows = hidden.shape[0]
    query_count = GROUPS * QUERIES
    raw_self = low_back(linear(hidden, self_weight))
    queries = low(raw_self[..., :D] + self_bias[0])
    self_keys = low(raw_self[..., D:2 * D])
    values = low(raw_self[..., 2 * D:] + self_bias[1])
    scores = low_back(jnp.einsum('bqhd,bkhd->bhqk', heads_of(queries), heads_of(self_keys), precision=highest)) * score_scale
    visible = (segment[:, :, None] == segment[:, None, :])[:, None]
    weights = jax.nn.softmax(jnp.where(visible, scores, masked_score), axis=-1)
    attended = jnp.einsum('bhqk,bkhd->bqhd', low(weights), heads_of(values), precision=highest)
    attended = low(low_back(attended.reshape(hidden.shape)))
    first_out = layer_norm(hidden + low_back(linear(attended, output_weight)) + self_bias[2], norm_gain[0], norm_shift[0])
    first_low = low(first_out)
    cross_query = low(low_back(linear(first_low[:, :query_count], query_weight)) + cross_bias[0])
    select = (image_order[:, :, None] == jnp.arange(GROUPS, dtype=jnp.int32)[None, None, :]).astype(jnp.float32)
    by_image = jnp.einsum('bgm,bgqd->bmqd', select, cross_query.reshape(batch_rows, GROUPS, QUERIES, D), precision=highest)
    raw_image = low_back(linear(images, image_weight))
    image_keys = low(raw_image[..., :D])
    image_values = low(raw_image[..., D:] + cross_bias[1])
    cross_scores = low_back(jnp.einsum('bmqhd,bmphd->bmhqp', heads_of(by_image), heads_of(image_keys), precision=highest)) * score_scale
    patch_valid = jnp.arange(PATCHES, dtype=jnp.int32) < PATCHES - PAD
    cross_probs = jax.nn.softmax(jnp.where(patch_valid, cross_scores, masked_score), axis=-1)
    cross_out = jnp.einsum('bmhqp,bmphd->bmqhd', low(cross_probs), heads_of(image_values), precision=highest)
    cross_out = low(low_back(cross_out.reshape(batch_rows, GROUPS, QUERIES, D)))
    by_group = jnp.einsum('bgm,bmqd->bgqd', select, cross_out, precision=highest).reshape(batch_rows, query_count, D)
    second = layer_norm(first_out[:, :query_count] + low_back(linear(by_group, cross_weight)) + cross_bias[2], norm_gain[1], norm_shift[1])

    def feed_forward(inputs, residual, branch):
        offset = branch * FF
        preact = low_back(linear(inputs, expand_weight[:, offset:offset + FF])) + expand_bias[offset:offset + FF]
        active = low(jax.nn.gelu(preact, approximate=False))
        summed = residual + low_back(linear(active, reduce_weight[offset:offset + FF])) + reduce_bias[branch]
        return layer_norm(summed, norm_gain[2 + branch], norm_shift[2 + branch])
    query_final = feed_forward(low(second), second, 0)
    text_final = feed_forward(first_low[:, query_count:], first_out[:, query_count:], 1)
    return jnp.concatenate([query_final, text_final], axis=1)

def reference(hidden, lengths, image_order, features, cotangent, self_weight, output_weight, self_bias, norm_gain, norm_shift, query_weight, image_weight, cross_weight, cross_bias, expand_weight, expand_bias, reduce_weight, reduce_bias):
    params = tuple((tensor.astype(jnp.float32) for tensor in (self_weight, output_weight, self_bias, norm_gain, norm_shift, query_weight, image_weight, cross_weight, cross_bias, expand_weight, expand_bias, reduce_weight, reduce_bias)))
    block_rows = math.gcd(ROWS, 16)
    block_count = ROWS // block_rows
    segment = segments(lengths).reshape(block_count, block_rows, SEQ)
    orders = image_order.reshape(block_count, block_rows, GROUPS)
    images = features.reshape(block_count, block_rows, GROUPS, PATCHES, IMAGE_WIDTH)
    checked = jax.checkpoint(layer)

    def whole_layer(weights, inputs):

        def one_block(parts):
            return checked(weights, parts[0], parts[1], parts[2], parts[3].astype(jnp.float32))
        outputs = lax.map(one_block, (inputs.reshape(block_count, block_rows, SEQ, D), segment, orders, images))
        return outputs.reshape(ROWS, SEQ, D)
    mixed, pullback = jax.vjp(whole_layer, params, hidden.astype(jnp.float32))
    grads, hidden_gradient = pullback(cotangent.astype(jnp.float32))
    return (mixed.astype(jnp.bfloat16), hidden_gradient.astype(jnp.bfloat16), grads[0], grads[1], grads[2], grads[3], grads[4], grads[5], grads[6], grads[7], grads[8], grads[9], grads[10], grads[11], grads[12])
```

```python
import functools

import jax
import jax.numpy as jnp
from jax import lax
from jax.experimental import pallas as pl
from jax.experimental.pallas import tpu as pltpu
from jax.sharding import PartitionSpec as P

HEADS = 12
QUERIES = 32
GROUPS = 4
TEXT = 128
PATCHES = 264
PAD = 7

epsilon = 1e-06
masked_score = -1000000000.0

F32 = jnp.float32
BF16 = jnp.bfloat16
WIDE = 256
CHUNK = 768
VMEM = 56 * 2**20


def nn(left, right):
    return lax.dot_general(left, right, (((1,), (0,)), ((), ())), preferred_element_type=F32)


def nt(left, right):
    return lax.dot_general(left, right, (((1,), (1,)), ((), ())), preferred_element_type=F32)


def tn(left, right):
    return lax.dot_general(left, right, (((0,), (0,)), ((), ())), preferred_element_type=F32)


def norm(hidden):
    row_mean = jnp.mean(hidden, axis=-1, keepdims=True)
    centered = hidden - row_mean
    inverse = lax.rsqrt(jnp.mean(centered * centered, axis=-1, keepdims=True) + epsilon)
    return centered * inverse, inverse


def norm_backward(slopes, normed, inverse, gain):
    scaled = slopes * gain
    return inverse * (
        scaled
        - jnp.mean(scaled, axis=-1, keepdims=True)
        - normed * jnp.mean(scaled * normed, axis=-1, keepdims=True)
    )


def total(values):
    return jnp.sum(values, axis=0, keepdims=True)


def iota(shape, axis):
    return lax.broadcasted_iota(jnp.int32, shape, axis)


def only_head(values, head):
    lanes = iota(values.shape, 1) >> 6
    return jnp.where(lanes == head, values, jnp.zeros_like(values))


def whole(shape):
    return pl.BlockSpec(shape, lambda *_: (0,) * len(shape))


def params(steps):
    return pltpu.CompilerParams(
        dimension_semantics=("arbitrary",) * steps, vmem_limit_bytes=VMEM
    )


def same_group(lengths, row, sequence):
    first = lengths[row, 0]
    second = first + lengths[row, 1]
    third = second + lengths[row, 2]

    def group(place):
        text = place - GROUPS * QUERIES
        after = (
            (text >= first).astype(jnp.int32)
            + (text >= second).astype(jnp.int32)
            + (text >= third).astype(jnp.int32)
        )
        return jnp.where(text < 0, place >> 5, after)

    keys = group(iota((sequence, 1), 0))
    queries = group(iota((1, sequence), 1))
    return jnp.where(keys == queries, 0.0, masked_score).astype(F32)


def self_forward_kernel(
    lengths, order, x_ref, ws_ref, wo_ref, wq_ref, sb_ref, gain_ref, shift_ref, cb_ref,
    qkv_ref, att_ref, lse_ref, n_ref, inv_ref, low_ref, cq_ref, bias_ref,
):
    row = pl.program_id(0)
    x = x_ref[0]
    sequence, width = x.shape
    bias_ref[...] = same_group(lengths, row, sequence)
    qkv_ref[0, :, :width] = (nn(x, ws_ref[:, :width]) + sb_ref[0:1]).astype(BF16)
    qkv_ref[0, :, width : 2 * width] = nn(x, ws_ref[:, width : 2 * width]).astype(BF16)
    qkv_ref[0, :, 2 * width :] = (nn(x, ws_ref[:, 2 * width :]) + sb_ref[1:2]).astype(BF16)
    scale = (width // HEADS) ** -0.5
    for part in range(width // WIDE):
        at = part * WIDE
        queries = qkv_ref[0, :, at : at + WIDE] * jnp.asarray(scale, BF16)
        keys = qkv_ref[0, :, width + at : width + at + WIDE]
        values = qkv_ref[0, :, 2 * width + at : 2 * width + at + WIDE]
        out = jnp.zeros((sequence, WIDE), F32)
        for head in range(4):
            scores = nt(keys, only_head(queries, head)) + bias_ref[...]
            top = jnp.max(scores, axis=0, keepdims=True)
            weights = jnp.exp(scores - top)
            mass = total(weights)
            lse_ref[0, 4 * part + head : 4 * part + head + 1] = top + jnp.log(mass)
            out += tn((weights * (1.0 / mass)).astype(BF16), only_head(values, head))
        att_ref[0, :, at : at + WIDE] = out.astype(BF16)
    normed, inverse = norm(x.astype(F32) + nn(att_ref[0], wo_ref[...]) + sb_ref[2:3])
    n_ref[0] = normed
    inv_ref[0] = inverse
    low_ref[0] = (normed * gain_ref[0:1] + shift_ref[0:1]).astype(BF16)
    cq = (nn(low_ref[0, : GROUPS * QUERIES], wq_ref[...]) + cb_ref[0:1]).astype(BF16)
    for group in range(GROUPS):
        to = pl.multiple_of(order[row, group] * QUERIES, QUERIES)
        cq_ref[0, pl.ds(to, QUERIES)] = cq[group * QUERIES : (group + 1) * QUERIES]


def self_forward(lengths, order, hidden, ws, wo, wq, sb, gain, shift, cb):
    rows, sequence, width = hidden.shape

    def by_row(*shape):
        return pl.BlockSpec((1, *shape), lambda r, *_: (r,) + (0,) * len(shape))

    def out(dtype, *shape):
        return jax.ShapeDtypeStruct((rows, *shape), dtype)

    queries = GROUPS * QUERIES
    return pl.pallas_call(
        self_forward_kernel,
        grid_spec=pltpu.PrefetchScalarGridSpec(
            num_scalar_prefetch=2,
            grid=(rows,),
            in_specs=[by_row(sequence, width)]
            + [whole(a.shape) for a in (ws, wo, wq, sb, gain, shift, cb)],
            out_specs=[
                by_row(sequence, 3 * width),
                by_row(sequence, width),
                by_row(HEADS, sequence),
                by_row(sequence, width),
                by_row(sequence, 1),
                by_row(sequence, width),
                by_row(queries, width),
            ],
            scratch_shapes=[pltpu.VMEM((sequence, sequence), F32)],
        ),
        out_shape=[
            out(BF16, sequence, 3 * width),
            out(BF16, sequence, width),
            out(F32, HEADS, sequence),
            out(F32, sequence, width),
            out(F32, sequence, 1),
            out(BF16, sequence, width),
            out(BF16, queries, width),
        ],
        compiler_params=params(1),
        cost_estimate=pl.CostEstimate(
            flops=2 * rows * sequence * width * 5 * width, bytes_accessed=10**7, transcendentals=0
        ),
        name="self_forward",
    )(lengths, order, hidden, ws, wo, wq, sb, gain, shift, cb)


def image_kernel(slots, x_ref, w_ref, cb_ref, kv_ref, packed_ref):
    count = x_ref.shape[2]
    width = w_ref.shape[1] // 2

    @pl.when(pl.program_id(0) == 0)
    def _():
        packed_ref[...] = jnp.zeros_like(packed_ref)

    for image in range(GROUPS):
        packed_ref[image * slots : image * slots + count] = x_ref[0, image]
    kv_ref[0, :, :width] = nn(packed_ref[...], w_ref[:, :width]).astype(BF16)
    kv_ref[0, :, width:] = (nn(packed_ref[...], w_ref[:, width:]) + cb_ref[1:2]).astype(BF16)


def image_forward(features, weight, cb, slots):
    rows, images, count, depth = features.shape
    width = weight.shape[1]
    return pl.pallas_call(
        functools.partial(image_kernel, slots),
        grid=(rows,),
        in_specs=[
            pl.BlockSpec((1, images, count, depth), lambda r: (r, 0, 0, 0)),
            whole(weight.shape),
            whole(cb.shape),
        ],
        out_specs=pl.BlockSpec((1, images * slots, width), lambda r: (r, 0, 0)),
        out_shape=jax.ShapeDtypeStruct((rows, images * slots, width), BF16),
        scratch_shapes=[pltpu.VMEM((images * slots, depth), BF16)],
        compiler_params=params(1),
        cost_estimate=pl.CostEstimate(
            flops=2 * rows * images * slots * depth * width, bytes_accessed=10**7, transcendentals=0
        ),
        name="image_forward",
    )(features, weight, cb)


def unused_slots(place, slots, local_count):
    patch = place[1] * local_count + iota((slots, 1), 0)
    used = (iota((slots, 1), 0) < local_count) & (patch < PATCHES - PAD)
    return jnp.where(used, 0.0, masked_score).astype(F32)


def spread_heads(values):
    return jnp.concatenate([only_head(values, head) for head in range(4)], axis=0)


def gather_heads(values):
    rows = values.shape[0] // 4
    result = only_head(values[:rows], 0)
    for head in range(1, 4):
        result += only_head(values[head * rows : (head + 1) * rows], head)
    return result


def cross_forward_kernel(slots, local_count, place, kv_ref, q_ref, o_ref, st_ref):
    width = q_ref.shape[2]
    scale = (width // HEADS) ** -0.5
    unused = unused_slots(place, slots, local_count)
    for image in range(GROUPS):
        rows = slice(image * slots, (image + 1) * slots)
        here = slice(image * QUERIES, (image + 1) * QUERIES)
        scores = []
        for part in range(width // WIDE):
            lanes = slice(part * WIDE, (part + 1) * WIDE)
            queries = q_ref[0, here, lanes] * jnp.asarray(scale, BF16)
            scores.append(nt(kv_ref[0, rows, lanes], spread_heads(queries)))
        scores = jnp.concatenate(scores, axis=1) + unused
        top = jnp.max(scores, axis=0, keepdims=True)
        weights = jnp.exp(scores - top)
        mass = total(weights)
        st_ref[0, image : image + 1] = top
        st_ref[0, GROUPS + image : GROUPS + image + 1] = mass
        probs = (weights * (1.0 / mass)).astype(BF16)
        for part in range(width // WIDE):
            lanes = slice(part * WIDE, (part + 1) * WIDE)
            values = kv_ref[0, rows, width + part * WIDE : width + (part + 1) * WIDE]
            block = slice(part * 4 * QUERIES, (part + 1) * 4 * QUERIES)
            o_ref[0, here, lanes] = gather_heads(tn(probs[:, block], values)).astype(BF16)


def cross_forward(place, kv, queries, slots, local_count):
    rows, length, width = queries.shape
    lanes = HEADS * QUERIES
    return pl.pallas_call(
        functools.partial(cross_forward_kernel, slots, local_count),
        grid_spec=pltpu.PrefetchScalarGridSpec(
            num_scalar_prefetch=1,
            grid=(rows,),
            in_specs=[
                pl.BlockSpec((1, *kv.shape[1:]), lambda r, place: (place[0] + r, 0, 0)),
                pl.BlockSpec((1, length, width), lambda r, _: (r, 0, 0)),
            ],
            out_specs=[
                pl.BlockSpec((1, length, width), lambda r, _: (r, 0, 0)),
                pl.BlockSpec((1, 2 * GROUPS, lanes), lambda r, _: (r, 0, 0)),
            ],
        ),
        out_shape=[
            jax.ShapeDtypeStruct((rows, length, width), BF16),
            jax.ShapeDtypeStruct((rows, 2 * GROUPS, lanes), F32),
        ],
        compiler_params=params(1),
        cost_estimate=pl.CostEstimate(
            flops=rows * 2 * 10**9, bytes_accessed=rows * 2 * 10**6, transcendentals=0
        ),
        name="cross_forward",
    )(place, kv, queries)


def cross_backward_kernel(
    slots, local_count, place, kv_ref, q_ref, do_ref, ld_ref, dq_ref, dkv_ref, sum_ref
):
    width = q_ref.shape[2]
    scale = (width // HEADS) ** -0.5
    unused = unused_slots(place, slots, local_count)

    @pl.when(pl.program_id(0) == 0)
    def _():
        sum_ref[...] = jnp.zeros_like(sum_ref)

    for image in range(GROUPS):
        rows = slice(image * slots, (image + 1) * slots)
        here = slice(image * QUERIES, (image + 1) * QUERIES)
        lse = ld_ref[0, image : image + 1]
        delta = ld_ref[0, GROUPS + image : GROUPS + image + 1]
        for part in range(width // WIDE):
            lanes = slice(part * WIDE, (part + 1) * WIDE)
            vlanes = slice(width + part * WIDE, width + (part + 1) * WIDE)
            block = slice(part * 4 * QUERIES, (part + 1) * 4 * QUERIES)
            queries = spread_heads(q_ref[0, here, lanes])
            slopes = spread_heads(do_ref[0, here, lanes])
            keys = kv_ref[0, rows, lanes]
            values = kv_ref[0, rows, vlanes]
            scores = nt(keys, queries * jnp.asarray(scale, BF16)) + unused
            probs = jnp.exp(scores - lse[:, block])
            prob_slopes = nt(values, slopes)
            low = (probs * (prob_slopes - delta[:, block]) * scale).astype(BF16)
            value_slope = nn(probs.astype(BF16), slopes)
            sum_ref[:, lanes] += total(value_slope)
            dkv_ref[0, rows, lanes] = nn(low, queries).astype(BF16)
            dkv_ref[0, rows, vlanes] = value_slope.astype(BF16)
            dq_ref[0, here, lanes] = gather_heads(tn(low, keys)).astype(BF16)


def cross_backward(place, kv, queries, slopes, ld, slots, local_count):
    rows, length, width = queries.shape
    lanes = HEADS * QUERIES
    by_row = pl.BlockSpec((1, length, width), lambda r, _: (r, 0, 0))
    return pl.pallas_call(
        functools.partial(cross_backward_kernel, slots, local_count),
        grid_spec=pltpu.PrefetchScalarGridSpec(
            num_scalar_prefetch=1,
            grid=(rows,),
            in_specs=[
                pl.BlockSpec((1, *kv.shape[1:]), lambda r, place: (place[0] + r, 0, 0)),
                by_row,
                by_row,
                pl.BlockSpec((1, 2 * GROUPS, lanes), lambda r, _: (r, 0, 0)),
            ],
            out_specs=[
                by_row,
                pl.BlockSpec((1, *kv.shape[1:]), lambda r, _: (r, 0, 0)),
                pl.BlockSpec((1, width), lambda r, _: (0, 0)),
            ],
        ),
        out_shape=[
            jax.ShapeDtypeStruct((rows, length, width), BF16),
            jax.ShapeDtypeStruct((rows, *kv.shape[1:]), BF16),
            jax.ShapeDtypeStruct((1, width), F32),
        ],
        compiler_params=params(1),
        cost_estimate=pl.CostEstimate(
            flops=rows * 4 * 10**9, bytes_accessed=rows * 4 * 10**6, transcendentals=0
        ),
        name="cross_backward",
    )(place, kv, queries, slopes, ld)


def feed_forward_step(ffn, step, z, we, be, wr):
    act_ref, slope_ref, sum_ref = ffn
    pre = nn(z, we) + be
    phi = 0.5 * (1.0 + lax.erf(pre * 0.7071067811865476))
    act = (pre * phi).astype(BF16)
    act_ref[:, pl.ds(pl.multiple_of(step * CHUNK, 128), CHUNK)] = act
    slope_ref[step] = phi + pre * jnp.exp(-0.5 * pre * pre) * 0.3989422804014327
    part = nn(act, wr)

    @pl.when(step == 0)
    def _():
        sum_ref[...] = part

    @pl.when(step > 0)
    def _():
        sum_ref[...] += part


def feed_backward_step(stack_ref, be_slope_ref, slope_ref, sum_ref, step, first, dh_low, we, wr, at):
    pre_slope = nt(dh_low, wr) * slope_ref[step]
    lanes = pl.multiple_of(step * CHUNK, 128)
    be_slope_ref[:, pl.ds(lanes, CHUNK)] = total(pre_slope)
    low = pre_slope.astype(BF16)
    stack_ref[:, pl.ds(at + lanes, CHUNK)] = low
    part = nt(low, we)

    @pl.when(first)
    def _():
        sum_ref[...] = part

    @pl.when(jnp.logical_not(first))
    def _():
        sum_ref[...] += part


def text_kernel(
    n_ref, low_ref, cot_ref, we_ref, be_ref, wr_ref, br_ref, gain_ref, shift_ref,
    mixed_ref, stack_ref, dz_ref, be_slope_ref, vec_ref, slope_ref, sum_ref, dh_ref,
):
    phase, step = pl.program_id(0), pl.program_id(1)
    steps = pl.num_programs(1)
    rows, length, width = n_ref.shape
    inner = be_slope_ref.shape[1]
    tokens = rows * length
    z = low_ref[...].reshape(tokens, width)

    @pl.when(phase == 0)
    def _():
        feed_forward_step(
            (stack_ref, slope_ref, sum_ref), step, z, we_ref[...], be_ref[...], wr_ref[...]
        )

    @pl.when((phase == 1) & (step == 0))
    def _():
        stack_ref[:, 2 * inner : 2 * inner + width] = z
        residual = n_ref[...].reshape(tokens, width) * gain_ref[0:1] + shift_ref[0:1]
        normed, inverse = norm(residual + sum_ref[...] + br_ref[1:2])
        mixed = normed * gain_ref[3:4] + shift_ref[3:4]
        mixed_ref[...] = mixed.astype(BF16).reshape(rows, length, width)
        slopes = cot_ref[...].reshape(tokens, width).astype(F32)
        dh = norm_backward(slopes, normed, inverse, gain_ref[3:4])
        vec_ref[...] = jnp.zeros_like(vec_ref)
        vec_ref[0:1] = total(dh)
        vec_ref[1:2] = total(slopes * normed)
        vec_ref[2:3] = total(slopes)
        dh_ref[...] = dh
        stack_ref[:, 2 * inner + width : 2 * inner + 2 * width] = dh.astype(BF16)

    @pl.when(phase == 1)
    def _():
        feed_backward_step(
            stack_ref, be_slope_ref, slope_ref, sum_ref, steps - 1 - step, step == 0,
            stack_ref[:, 2 * inner + width : 2 * inner + 2 * width], we_ref[...], wr_ref[...], inner,
        )

    @pl.when((phase == 1) & (step == steps - 1))
    def _():
        dz_ref[...] = (dh_ref[...] + sum_ref[...]).reshape(rows, length, width)


def branch_specs(branch, steps, width):
    def turn(phase, step):
        return branch * steps + jnp.where(phase == 0, step, steps - 1 - step)

    return [
        pl.BlockSpec((width, CHUNK), lambda p, s, *_: (0, turn(p, s))),
        pl.BlockSpec((1, CHUNK), lambda p, s, *_: (0, turn(p, s))),
        pl.BlockSpec((CHUNK, width), lambda p, s, *_: (turn(p, s), 0)),
    ]


def text_branch(n1, low1, cot, we, be, wr, br, gain, shift):
    rows, sequence, width = n1.shape
    inner = we.shape[1] // 2
    steps = inner // CHUNK
    tokens = rows * TEXT
    half = pl.BlockSpec((rows, TEXT, width), lambda *_: (0, 1, 0))
    wide = 2 * inner + 2 * width
    return pl.pallas_call(
        text_kernel,
        grid=(2, steps),
        in_specs=[half, half, half]
        + branch_specs(1, steps, width)
        + [whole(br.shape), whole(gain.shape), whole(shift.shape)],
        out_specs=[
            half,
            whole((tokens, wide)),
            whole((rows, TEXT, width)),
            whole((1, inner)),
            whole((8, width)),
        ],
        out_shape=[
            jax.ShapeDtypeStruct((rows, sequence, width), BF16),
            jax.ShapeDtypeStruct((tokens, wide), BF16),
            jax.ShapeDtypeStruct((rows, TEXT, width), F32),
            jax.ShapeDtypeStruct((1, inner), F32),
            jax.ShapeDtypeStruct((8, width), F32),
        ],
        scratch_shapes=[
            pltpu.VMEM((steps, tokens, CHUNK), F32),
            pltpu.VMEM((tokens, width), F32),
            pltpu.VMEM((tokens, width), F32),
        ],
        compiler_params=params(2),
        cost_estimate=pl.CostEstimate(
            flops=16 * tokens * width * inner, bytes_accessed=2 * 10**7, transcendentals=0
        ),
        name="text_branch",
    )(n1, low1, cot, we, be, wr, br, gain, shift)


def head_map(width):
    shape = (HEADS * QUERIES, width)
    return (iota(shape, 0) // QUERIES == iota(shape, 1) // (width // HEADS)).astype(BF16)


def own_query(tokens):
    shape = (tokens, HEADS * QUERIES)
    return (iota(shape, 0) & (QUERIES - 1)) == (iota(shape, 1) & (QUERIES - 1))


def two_terms(values):
    high = values.astype(BF16)
    return high, (values - high.astype(F32)).astype(BF16)


def query_kernel(
    order, o_ref, po_ref, st_ref, pst_ref, n_ref, cot_ref, we_ref, be_ref, wr_ref, br_ref,
    gain_ref, shift_ref, wx_ref, cb_ref, _,
    mixed_ref, stack_ref, dh2_ref, dca_ref, ld_ref, be_slope_ref, vec_ref,
    slope_ref, sum_ref, dh_ref, out_ref, x2_ref, n2_ref, inv2_ref, map_ref,
):
    phase, step = pl.program_id(0), pl.program_id(1)
    steps = pl.num_programs(1)
    rows, length, width = n_ref.shape
    inner = be_slope_ref.shape[1]
    tokens = rows * length
    zs = slice(2 * inner, 2 * inner + width)
    dhs = slice(2 * inner + width, 2 * inner + 2 * width)
    cas = slice(2 * inner + 2 * width, 2 * inner + 3 * width)
    dh2s = slice(2 * inner + 3 * width, 2 * inner + 4 * width)

    @pl.when((phase == 0) & (step == 0))
    def _():
        map_ref[...] = head_map(width)
        shares, other_shares = [], []
        for row in range(rows):
            top, other_top = st_ref[row, :GROUPS], pst_ref[row, :GROUPS]
            both = jnp.maximum(top, other_top)
            mass = st_ref[row, GROUPS:] * jnp.exp(top - both)
            other_mass = pst_ref[row, GROUPS:] * jnp.exp(other_top - both)
            everything = mass + other_mass
            ld_ref[row, :GROUPS] = both + jnp.log(everything)
            inverse = 1.0 / everything
            for image in range(GROUPS):
                at = slice(image, image + 1)
                wide = (QUERIES, HEADS * QUERIES)
                shares.append(jnp.broadcast_to((mass * inverse)[at], wide))
                other_shares.append(jnp.broadcast_to((other_mass * inverse)[at], wide))
        own = own_query(tokens)

        def spread(parts):
            high, rest = two_terms(jnp.where(own, jnp.concatenate(parts, axis=0), 0.0))
            return nn(high, map_ref[...]) + nn(rest, map_ref[...])

        out_ref[...] = spread(shares) * o_ref[...].reshape(tokens, width).astype(F32) + spread(
            other_shares
        ) * po_ref[...].reshape(tokens, width).astype(F32)
        for row in range(rows):
            for group in range(GROUPS):
                to = row * length + group * QUERIES
                at = pl.multiple_of(row * length + order[row, group] * QUERIES, QUERIES)
                stack_ref[to : to + QUERIES, cas] = out_ref[pl.ds(at, QUERIES)].astype(BF16)
        residual = n_ref[...].reshape(tokens, width) * gain_ref[0:1] + shift_ref[0:1]
        normed, inverse = norm(residual + nn(stack_ref[:, cas], wx_ref[...]) + cb_ref[2:3])
        n2_ref[...] = normed
        inv2_ref[...] = inverse
        x2 = normed * gain_ref[1:2] + shift_ref[1:2]
        x2_ref[...] = x2
        stack_ref[:, zs] = x2.astype(BF16)

    @pl.when(phase == 0)
    def _():
        feed_forward_step(
            (stack_ref, slope_ref, sum_ref), step, stack_ref[:, zs], we_ref[...], be_ref[...],
            wr_ref[...],
        )

    @pl.when((phase == 1) & (step == 0))
    def _():
        normed, inverse = norm(x2_ref[...] + sum_ref[...] + br_ref[0:1])
        mixed = normed * gain_ref[2:3] + shift_ref[2:3]
        mixed_ref[...] = mixed.astype(BF16).reshape(rows, length, width)
        slopes = cot_ref[...].reshape(tokens, width).astype(F32)
        dh = norm_backward(slopes, normed, inverse, gain_ref[2:3])
        vec_ref[...] = jnp.zeros_like(vec_ref)
        vec_ref[0:1] = total(dh)
        vec_ref[1:2] = total(slopes * normed)
        vec_ref[2:3] = total(slopes)
        dh_ref[...] = dh
        stack_ref[:, dhs] = dh.astype(BF16)

    @pl.when(phase == 1)
    def _():
        feed_backward_step(
            stack_ref, be_slope_ref, slope_ref, sum_ref, steps - 1 - step, step == 0,
            stack_ref[:, dhs], we_ref[...], wr_ref[...], inner,
        )

    @pl.when((phase == 1) & (step == steps - 1))
    def _():
        dz = dh_ref[...] + sum_ref[...]
        normed = n2_ref[...]
        dh2 = norm_backward(dz, normed, inv2_ref[...], gain_ref[1:2])
        vec_ref[3:4] = total(dz * normed)
        vec_ref[4:5] = total(dz)
        vec_ref[5:6] = total(dh2)
        dh2_ref[...] = dh2.reshape(rows, length, width)
        low = dh2.astype(BF16)
        stack_ref[:, dh2s] = low
        dca = nt(low, wx_ref[...]).astype(BF16)
        for row in range(rows):
            for group in range(GROUPS):
                at = row * length + group * QUERIES
                to = pl.multiple_of(order[row, group] * QUERIES, QUERIES)
                dca_ref[row, pl.ds(to, QUERIES)] = dca[at : at + QUERIES]
        high, rest = two_terms(
            dca_ref[...].reshape(tokens, width).astype(F32) * out_ref[...]
        )
        delta = jnp.where(own_query(tokens), nt(high, map_ref[...]) + nt(rest, map_ref[...]), 0.0)
        for row in range(rows):
            for image in range(GROUPS):
                at = row * length + image * QUERIES
                ld_ref[row, GROUPS + image : GROUPS + image + 1] = total(delta[at : at + QUERIES])


def query_branch(
    order, o, po, st, pst, n1, cot, we, be, wr, br, gain, shift, wx, cb, mixed
):
    rows, sequence, width = n1.shape
    inner = we.shape[1] // 2
    steps = inner // CHUNK
    length = GROUPS * QUERIES
    tokens = rows * length
    half = pl.BlockSpec((rows, length, width), lambda *_: (0, 0, 0))
    wide = 2 * inner + 4 * width
    lanes = HEADS * QUERIES
    return pl.pallas_call(
        query_kernel,
        grid_spec=pltpu.PrefetchScalarGridSpec(
            num_scalar_prefetch=1,
            grid=(2, steps),
            in_specs=[whole(a.shape) for a in (o, po, st, pst)]
            + [half, half]
            + branch_specs(0, steps, width)
            + [whole(a.shape) for a in (br, gain, shift, wx, cb)]
            + [pl.BlockSpec(memory_space=pl.ANY)],
            out_specs=[
                half,
                whole((tokens, wide)),
                whole((rows, length, width)),
                whole((rows, length, width)),
                whole((rows, 2 * GROUPS, lanes)),
                whole((1, inner)),
                whole((8, width)),
            ],
            scratch_shapes=[
                pltpu.VMEM((steps, tokens, CHUNK), F32),
                pltpu.VMEM((tokens, width), F32),
                pltpu.VMEM((tokens, width), F32),
                pltpu.VMEM((tokens, width), F32),
                pltpu.VMEM((tokens, width), F32),
                pltpu.VMEM((tokens, width), F32),
                pltpu.VMEM((tokens, 1), F32),
                pltpu.VMEM((lanes, width), BF16),
            ],
        ),
        out_shape=[
            jax.ShapeDtypeStruct((rows, sequence, width), BF16),
            jax.ShapeDtypeStruct((tokens, wide), BF16),
            jax.ShapeDtypeStruct((rows, length, width), F32),
            jax.ShapeDtypeStruct((rows, length, width), BF16),
            jax.ShapeDtypeStruct((rows, 2 * GROUPS, lanes), F32),
            jax.ShapeDtypeStruct((1, inner), F32),
            jax.ShapeDtypeStruct((8, width), F32),
        ],
        input_output_aliases={15: 0},
        compiler_params=params(2),
        cost_estimate=pl.CostEstimate(
            flops=18 * tokens * width * inner, bytes_accessed=2 * 10**7, transcendentals=0
        ),
        name="query_branch",
    )(order, o, po, st, pst, n1, cot, we, be, wr, br, gain, shift, wx, cb, mixed)


def self_backward_kernel(
    lengths, order, dcq_ref, pdcq_ref, dh2_ref, dz_ref, n_ref, inv_ref, qkv_ref, lse_ref,
    ws_ref, wo_ref, wq_ref, gain_ref,
    grad_ref, dqkv_ref, low_ref, dcq_low_ref, vec_ref, dcq_sum, dx_ref, datt_ref, bias_ref,
):
    row = pl.program_id(0)
    sequence, width = n_ref.shape[1:]
    length = GROUPS * QUERIES

    @pl.when(row == 0)
    def _():
        vec_ref[...] = jnp.zeros_like(vec_ref)

    bias_ref[...] = same_group(lengths, row, sequence)
    dcq = dcq_ref[0].astype(F32) + pdcq_ref[0].astype(F32)
    dcq_sum[...] = dcq
    vec_ref[0:1] += total(dcq)
    for group in range(GROUPS):
        at = pl.multiple_of(order[row, group] * QUERIES, QUERIES)
        dcq_low_ref[0, group * QUERIES : (group + 1) * QUERIES] = dcq_sum[
            pl.ds(at, QUERIES)
        ].astype(BF16)
    dx_ref[:length] = dh2_ref[0] + nt(dcq_low_ref[0], wq_ref[...])
    dx_ref[length:] = dz_ref[0]
    dx, normed = dx_ref[...], n_ref[0]
    vec_ref[1:2] += total(dx * normed)
    vec_ref[2:3] += total(dx)
    dh = norm_backward(dx, normed, inv_ref[0], gain_ref[0:1])
    vec_ref[3:4] += total(dh)
    dx_ref[...] = dh
    low_ref[0] = dh.astype(BF16)
    datt_ref[...] = nt(low_ref[0], wo_ref[...]).astype(BF16)
    scale = (width // HEADS) ** -0.5
    for part in range(width // WIDE):
        at = part * WIDE
        queries = qkv_ref[0, :, at : at + WIDE]
        keys = qkv_ref[0, :, width + at : width + at + WIDE]
        values = qkv_ref[0, :, 2 * width + at : 2 * width + at + WIDE]
        slopes = datt_ref[:, at : at + WIDE]
        dq = jnp.zeros((sequence, WIDE), F32)
        dk = jnp.zeros((sequence, WIDE), F32)
        dv = jnp.zeros((sequence, WIDE), F32)
        for head in range(4):
            own = only_head(queries, head)
            scores = nt(keys, own * jnp.asarray(scale, BF16)) + bias_ref[...]
            probs = jnp.exp(scores - lse_ref[0, 4 * part + head : 4 * part + head + 1])
            out_slopes = only_head(slopes, head)
            prob_slopes = nt(values, out_slopes)
            delta = total(probs * prob_slopes)
            low = (probs * (prob_slopes - delta) * scale).astype(BF16)
            dv += nn(probs.astype(BF16), out_slopes)
            dk += nn(low, own)
            dq += tn(low, only_head(keys, head))
        vec_ref[4:5, at : at + WIDE] += total(dq)
        vec_ref[5:6, at : at + WIDE] += total(dv)
        dqkv_ref[0, :, at : at + WIDE] = dq.astype(BF16)
        dqkv_ref[0, :, width + at : width + at + WIDE] = dk.astype(BF16)
        dqkv_ref[0, :, 2 * width + at : 2 * width + at + WIDE] = dv.astype(BF16)
    grad_ref[0] = (dx_ref[...] + nt(dqkv_ref[0], ws_ref[...])).astype(BF16)


def self_backward(lengths, order, dcq, pdcq, dh2, dz, n1, inv1, qkv, lse, ws, wo, wq, gain):
    rows, sequence, width = n1.shape
    length = GROUPS * QUERIES

    def by_row(*shape):
        return pl.BlockSpec((1, *shape), lambda r, *_: (r,) + (0,) * len(shape))

    def out(dtype, *shape):
        return jax.ShapeDtypeStruct((rows, *shape), dtype)

    return pl.pallas_call(
        self_backward_kernel,
        grid_spec=pltpu.PrefetchScalarGridSpec(
            num_scalar_prefetch=2,
            grid=(rows,),
            in_specs=[by_row(*a.shape[1:]) for a in (dcq, pdcq, dh2, dz, n1, inv1, qkv, lse)]
            + [whole(a.shape) for a in (ws, wo, wq, gain)],
            out_specs=[
                by_row(sequence, width),
                by_row(sequence, 3 * width),
                by_row(sequence, width),
                by_row(length, width),
                whole((8, width)),
            ],
            scratch_shapes=[
                pltpu.VMEM((length, width), F32),
                pltpu.VMEM((sequence, width), F32),
                pltpu.VMEM((sequence, width), BF16),
                pltpu.VMEM((sequence, sequence), F32),
            ],
        ),
        out_shape=[
            out(BF16, sequence, width),
            out(BF16, sequence, 3 * width),
            out(BF16, sequence, width),
            out(BF16, length, width),
            jax.ShapeDtypeStruct((8, width), F32),
        ],
        compiler_params=params(1),
        cost_estimate=pl.CostEstimate(
            flops=2 * rows * sequence * width * 9 * width, bytes_accessed=10**7, transcendentals=0
        ),
        name="self_backward",
    )(lengths, order, dcq, pdcq, dh2, dz, n1, inv1, qkv, lse, ws, wo, wq, gain)


def local(
    sizes,
    hidden,
    lengths,
    image_order,
    features,
    cotangent,
    self_weight,
    output_weight,
    self_bias,
    norm_gain,
    norm_shift,
    query_weight,
    image_weight,
    cross_weight,
    cross_bias,
    expand_weight,
    expand_bias,
    reduce_weight,
    reduce_bias,
):
    row_count, sequence, width = hidden.shape
    inner = reduce_weight.shape[0] // 2
    local_count = features.shape[2]
    slots = -(-local_count // 16) * 16
    length = GROUPS * QUERIES
    patch = lax.axis_index("patch").astype(jnp.int32)
    pair = sizes["patch"] == 2

    qkv, attended, lse, n1, inv1, low1, cq = self_forward(
        lengths, image_order, hidden, self_weight, output_weight, query_weight,
        self_bias, norm_gain, norm_shift, cross_bias,
    )

    def swap(array):
        return lax.ppermute(array, "patch", [(0, 1), (1, 0)])

    if pair:
        other_cq = swap(cq)
    else:
        other_cq = lax.all_gather(cq, "patch", axis=0, tiled=True)
    mixed, text_stack, dz_text, be_text, vec_text = text_branch(
        n1, low1, cotangent, expand_weight, expand_bias.reshape(1, -1), reduce_weight, reduce_bias,
        norm_gain, norm_shift,
    )
    kv = image_forward(features, image_weight, cross_bias, slots)
    if pair:
        here = jnp.stack([patch * row_count, patch])
        there = jnp.stack([(1 - patch) * row_count, patch])
        for_other, for_other_st = cross_forward(there, kv, other_cq, slots, local_count)
        po, pst = swap(for_other), swap(for_other_st)
        o, st = cross_forward(here, kv, cq, slots, local_count)
    else:
        here = jnp.stack([jnp.zeros_like(patch), patch])
        every_o, every_st = cross_forward(here, kv, other_cq, slots, local_count)
        top, mass = every_st[:, :GROUPS], every_st[:, GROUPS:]
        both = lax.pmax(top, "patch")
        mass = mass * jnp.exp(top - both)
        everything = lax.psum(mass, "patch")
        share = (mass / everything).reshape(-1, GROUPS, HEADS, QUERIES).transpose(0, 1, 3, 2)
        every_o = every_o.reshape(-1, GROUPS, QUERIES, HEADS, width // HEADS) * share[..., None]
        o = lax.psum_scatter(
            every_o.astype(BF16).reshape(-1, length, width), "patch", scatter_dimension=0, tiled=True
        )
        st = lax.dynamic_slice_in_dim(
            jnp.concatenate([both, everything], axis=1), patch * row_count, row_count, 0
        )
        po = jnp.zeros_like(o)
        pst = jnp.concatenate([st[:, :GROUPS], jnp.zeros_like(st[:, GROUPS:])], axis=1)
    mixed, query_stack, dh2, dca, ld, be_query, vec_query = query_branch(
        image_order, o, po, st, pst, n1, cotangent, expand_weight, expand_bias.reshape(1, -1),
        reduce_weight, reduce_bias, norm_gain, norm_shift, cross_weight, cross_bias, mixed,
    )
    if pair:
        other_dca, other_ld = swap(dca), swap(ld)
        dcq, dkv, dcv_sum = cross_backward(here, kv, cq, dca, ld, slots, local_count)
        for_other, other_dkv, other_sum = cross_backward(
            there, kv, other_cq, other_dca, other_ld, slots, local_count
        )
        pdcq = swap(for_other)
        dcv_sum = dcv_sum + other_sum
        own_first = patch == 0
        dkv = jnp.concatenate(
            [jnp.where(own_first, dkv, other_dkv), jnp.where(own_first, other_dkv, dkv)], axis=0
        )
    else:
        every_dca = lax.all_gather(dca, "patch", axis=0, tiled=True)
        every_ld = lax.all_gather(ld, "patch", axis=0, tiled=True)
        every_dcq, dkv, dcv_sum = cross_backward(
            here, kv, other_cq, every_dca, every_ld, slots, local_count
        )
        dcq = lax.psum_scatter(every_dcq, "patch", scatter_dimension=0, tiled=True)
        pdcq = jnp.zeros_like(dcq)
    grad, dqkv, dh1, dcq_low, vec_self = self_backward(
        lengths, image_order, dcq, pdcq, dh2, dz_text, n1, inv1, qkv, lse,
        self_weight, output_weight, query_weight, norm_gain,
    )

    def cut(stack, at, wide):
        return stack[:, at : at + wide]

    def flat(array):
        return array.reshape(-1, array.shape[-1])

    dkv_used = dkv.reshape(-1, slots, 2 * width)[:, :local_count].reshape(-1, 2 * width)
    gradients = [
        tn(flat(hidden), flat(dqkv)),
        tn(flat(attended), flat(dh1)),
        tn(flat(low1[:, :length]), flat(dcq_low)),
        tn(flat(features), dkv_used),
        tn(cut(query_stack, 2 * inner + 2 * width, width), cut(query_stack, 2 * inner + 3 * width, width)),
        jnp.concatenate(
            [tn(cut(s, 2 * inner, width), cut(s, inner, inner)) for s in (query_stack, text_stack)],
            axis=1,
        ),
        jnp.concatenate(
            [tn(cut(s, 0, inner), cut(s, 2 * inner + width, width)) for s in (query_stack, text_stack)],
            axis=0,
        ),
    ]

    def scatter(array):
        array = lax.psum_scatter(array.astype(BF16), "dp", scatter_dimension=0, tiled=True)
        array = lax.psum_scatter(array, "patch", scatter_dimension=1, tiled=True)
        return array.astype(F32)

    summed = [scatter(g) for g in gradients]
    vectors = lax.psum(
        (
            jnp.concatenate([vec_self[4:5], vec_self[5:6], vec_self[3:4]]),
            jnp.concatenate([vec_self[1:2], vec_query[3:4], vec_query[1:2], vec_text[1:2]]),
            jnp.concatenate([vec_self[2:3], vec_query[4:5], vec_query[2:3], vec_text[2:3]]),
            jnp.concatenate([vec_self[0:1], dcv_sum, vec_query[5:6]]),
            jnp.concatenate([be_query[0], be_text[0]]),
            jnp.concatenate([vec_query[0:1], vec_text[0:1]]),
        ),
        ("dp", "patch"),
    )
    return (
        mixed,
        grad,
        summed[0],
        summed[1],
        vectors[0],
        vectors[1],
        vectors[2],
        summed[2],
        summed[3],
        summed[4],
        vectors[3],
        summed[5],
        vectors[4],
        summed[6],
        vectors[5],
    )


def solution(mesh):
    rows = P(("dp", "patch"), None, None)
    counts = P(("dp", "patch"), None)
    matrix = P("dp", "patch")
    return jax.shard_map(
        functools.partial(local, dict(mesh.shape)),
        mesh=mesh,
        in_specs=(rows, counts, counts, P("dp", None, "patch", None), rows) + (P(),) * 13,
        out_specs=(
            rows, rows, matrix, matrix, P(), P(), P(), matrix, matrix, matrix, P(), matrix, P(),
            matrix, P(),
        ),
        check_vma=False,
    )
```
